32 devices in a mesh: grp: 2 (over x), pb: 8 (over z, y), ka: 2 (over core).
Axes of the slice: x: 2, y: 2, z: 4, core: 2. Of those that a mesh axis runs over, the one named last changes fastest.
Arguments:
- queries: bfloat16 [2048, 8192], P(('grp', 'pb', 'ka')), parts along dimension 0, may hold values from -2000 to 2000
- keys: bfloat16 [2048, 512], P(('grp', 'pb', 'ka')), parts along dimension 0, may hold values from -7 to 7
- values: bfloat16 [2048, 512], P(('grp', 'pb', 'ka')), parts along dimension 0, may hold values from -6 to 6
- panel_order: int32 [32], P('grp'), parts along dimension 0, may hold values from 0 to 15, as said below
- key_exp: int32 [32], P('grp'), parts along dimension 0, may hold values from -1 to 1
- value_exp: int32 [32], P('grp'), parts along dimension 0, may hold values from -1 to 1
Outputs:
- attended: bfloat16 [2048, 8192], P(('grp', 'pb', 'ka')), parts along dimension 0
The draws below stay inside these ranges and needn't reach their ends.
There are 2 independent parts, one for each index of `grp`. The reference program is written for one: setup_inputs(seed, part) draws one part's arguments, and reference() takes and returns one part's arrays. A program takes and returns all parts, laid end to end along the dimension named above; each array names one. Nothing has to cross between parts.
Inputs may be any that keep to these rules, and one draw needn't show every extreme that they name: panel_order is a permutation of the panel numbers 0 to 15.
All inputs are finite; a program needn't handle non-finite values.
Results may differ from the reference program's by a relative error of at most 0.005.
Values may be sent and summed in bfloat16 or wider, within the bound.
A program may use at most 128 MiB of HBM per device.

```python
import math
import jax
import jax.numpy as jnp
from jax import lax

HQ = 64
KVH = 4
HD = 128
KD = 64
PANELS = 16
QTOK = 1024
KEYS = 1024


def layout_tables(key):
    order = jax.random.permutation(jax.random.fold_in(key, 11), KEYS // KD).astype(jnp.int32)
    powers = jax.random.randint(jax.random.fold_in(key, 12), (KEYS // KD,), -1, 2, dtype=jnp.int32)
    return (order, powers)


def raw_keys(key):
    base = jnp.clip(jax.random.normal(jax.random.fold_in(key, 13), (KEYS, KVH * HD), jnp.float32), -6.0, 6.0)
    return base.astype(jnp.bfloat16).astype(jnp.float32)


def draw_keys(key, part):
    return raw_keys(key).astype(jnp.bfloat16)


def draw_panel_order(key, part):
    return layout_tables(key)[0]


def draw_key_exp(key, part):
    return layout_tables(key)[1]


def draw_queries(key, part):
    drawn = jnp.clip(jax.random.normal(jax.random.fold_in(key, 15), (QTOK, HQ * HD), jnp.float32), -6.0, 6.0)
    return drawn.astype(jnp.bfloat16)


def plant(result, key, smallest, top_value):
    place = [jax.random.randint(jax.random.fold_in(key, axis), (), 0, length) for axis, length in enumerate(result.shape)]
    widest = result.shape.index(max(result.shape))
    next_to = place[:widest] + [(place[widest] + 1) % result.shape[widest]] + place[widest + 1:]
    return result.at[tuple(place)].set(smallest).at[tuple(next_to)].set(top_value)


def block_scale(rng, extent, split, low, high):
    factor_of, own = 1.0, jax.random.fold_in(rng, 6)
    for axis_at, parts in split:
        draws = jnp.exp(jax.random.uniform(jax.random.fold_in(own, axis_at), (parts,), jnp.float32, low / len(split), high / len(split)))
        factor_of = factor_of * jnp.repeat(draws, extent[axis_at] // parts).reshape([-1 if axis == axis_at else 1 for axis in range(len(extent))])
    return factor_of


def gaussian(key, shape, spread, bound, cuts=(), held_as=jnp.bfloat16):
    entries = spread * jax.random.normal(key, shape, jnp.float32)
    if cuts:
        entries = entries * block_scale(key, shape, cuts, -0.22, 0.18)
    return jnp.clip(entries, -bound, bound).astype(held_as)


def setup_inputs(seed: int = 0, part: int = 0) -> dict:
    seeds = jax.random.split(jax.random.key(seed), 7)
    own_keys = jax.random.split(jax.random.fold_in(seeds[6], part), 7)
    queries = draw_queries(jax.random.fold_in(jax.random.fold_in(seeds[6], part), 71), part)
    keys = draw_keys(jax.random.fold_in(jax.random.fold_in(seeds[6], part), 71), part)
    values = gaussian(own_keys[2], (KEYS, KVH * HD), 1.0, 6.0, ((0, 16),))
    panel_order = draw_panel_order(jax.random.fold_in(jax.random.fold_in(seeds[6], part), 71), part)
    key_exp = draw_key_exp(jax.random.fold_in(jax.random.fold_in(seeds[6], part), 71), part)
    value_exp = plant(jax.random.randint(own_keys[5], (PANELS,), -1, 2), jax.random.fold_in(own_keys[5], 1), -1, 1).astype(jnp.int32)
    return {"queries": queries, "keys": keys, "values": values, "panel_order": panel_order, "key_exp": key_exp, "value_exp": value_exp}


NEG_BIG = -1.0e30


def reference(queries, keys, values, panel_order, key_exp, value_exp):
    panel_count = KEYS // KD
    key_scale = jnp.exp2(key_exp.astype(jnp.float32))
    value_scale = jnp.exp2(value_exp.astype(jnp.float32))
    key_eff = (keys.astype(jnp.float32).reshape(panel_count, KD, KVH * HD) * key_scale[:, None, None]).reshape(KEYS, KVH, HD)
    value_eff = (values.astype(jnp.float32).reshape(panel_count, KD, KVH * HD) * value_scale[:, None, None]).reshape(KEYS, KVH, HD)
    key_pos = (panel_order[:, None] * KD + jnp.arange(KD, dtype=jnp.int32)[None, :]).reshape(KEYS).astype(jnp.int32)
    block_rows = math.gcd(QTOK, 128)

    def one_block(first_row):
        rows_here = lax.dynamic_slice_in_dim(queries, first_row, block_rows, 0).astype(jnp.float32)
        rows_here = rows_here.reshape(block_rows, KVH, HQ // KVH, HD)
        scores = jnp.einsum("qgeh,kgh->qgek", rows_here, key_eff, precision=lax.Precision.HIGHEST) * (HD ** -0.5)
        query_pos = (KEYS - QTOK + first_row + jnp.arange(block_rows, dtype=jnp.int32)).astype(jnp.int32)
        visible = (key_pos[None, :] <= query_pos[:, None])[:, None, None, :]
        scores = jnp.where(visible, scores, NEG_BIG)
        top = jnp.max(scores, axis=-1, keepdims=True)
        weights = jnp.where(visible, jnp.exp(scores - top), 0.0)
        total = jnp.sum(weights, axis=-1)
        rounded = lax.optimization_barrier(weights.astype(jnp.bfloat16)).astype(jnp.float32)
        mixed = jnp.einsum("qgek,kgh->qgeh", rounded, value_eff, precision=lax.Precision.HIGHEST)
        return (mixed / total[..., None]).reshape(block_rows, HQ * HD).astype(jnp.bfloat16)

    starts = jnp.arange(0, QTOK, block_rows, dtype=jnp.int32)
    return lax.map(one_block, starts).reshape(QTOK, HQ * HD)
```

```python
import functools
import math

import jax
import jax.numpy as jnp
from jax import lax
from jax.experimental import pallas as pl
from jax.experimental.pallas import tpu as pltpu
from jax.sharding import PartitionSpec as P

HD = 128
NEG_BIG = -1e30
MESH = pl.DeviceIdType.MESH
TILE_HEADS = 8


def kernel(
    wide, q_hbm, k_hbm, v_hbm, order, key_exp, value_exp, o_hbm,
    qv, kv, ov, acc, top, vaug, in_sem, out_sem, send_sem, recv_sem,
):
    rows = qv.shape[0]
    panel = k_hbm.shape[0]
    width = k_hbm.shape[1]
    groups = width // HD
    per_group = qv.shape[1] // width
    outer = wide // 2
    block = 4 * panel
    pb, ka = lax.axis_index("pb"), lax.axis_index("ka")
    z, y = pb // 2, pb % 2

    def slot(zz, yy, kk):
        return (zz * 2 + yy) * 2 + kk

    def at(s):
        return kv.at[pl.ds(pl.multiple_of(s * panel, panel), panel)]

    def remote(s, way, to_pb, to_ka):
        return pltpu.make_async_remote_copy(
            src_ref=at(s), dst_ref=at(s), send_sem=send_sem.at[s, way], recv_sem=recv_sem.at[s],
            device_id={"pb": to_pb, "ka": to_ka}, device_id_type=MESH,
        )

    def each_way(zz, act):
        s = slot(zz, y, ka)

        @pl.when((zz <= z) & (z + 1 < outer))
        def _():
            act(remote(s, 0, jnp.minimum(pb + 2, wide - 1), ka))

        @pl.when((zz >= z) & (z >= 1))
        def _():
            act(remote(s, 1, jnp.maximum(pb - 2, 0), ka))

        act(remote(s, 2, z * 2 + 1 - y, ka))
        act(remote(s, 3, pb, 1 - ka))

    def across(zz):
        return remote(slot(zz, 1 - y, ka), 3, pb, 1 - ka)

    def arrived(s):
        remote(s, 3, pb, 1 - ka).wait_recv()

    def start(copy):
        copy.start()

    mine = slot(z, y, ka)
    k_in = pltpu.make_async_copy(k_hbm, at(mine).at[:, pl.ds(0, width)], in_sem.at[0])
    v_in = pltpu.make_async_copy(v_hbm, at(mine).at[:, pl.ds(width, width)], in_sem.at[1])
    q_in = pltpu.make_async_copy(q_hbm, qv, in_sem.at[2])
    k_in.start()
    v_in.start()
    q_in.start()

    barrier = pltpu.get_barrier_semaphore()
    pl.semaphore_signal(barrier, inc=1, device_id={"pb": pb, "ka": 1 - ka}, device_id_type=MESH)
    pl.semaphore_signal(
        barrier, inc=1, device_id={"pb": z * 2 + 1 - y, "ka": ka}, device_id_type=MESH
    )

    @pl.when(z + 1 < outer)
    def _():
        pl.semaphore_signal(
            barrier, inc=1, device_id={"pb": jnp.minimum(pb + 2, wide - 1), "ka": ka},
            device_id_type=MESH,
        )

    @pl.when(z >= 1)
    def _():
        pl.semaphore_signal(
            barrier, inc=1, device_id={"pb": jnp.maximum(pb - 2, 0), "ka": ka}, device_id_type=MESH
        )

    inside = (z + 1 < outer).astype(jnp.int32) + (z >= 1).astype(jnp.int32)
    pl.semaphore_wait(barrier, 2 + inside)

    k_in.wait()
    v_in.wait()
    each_way(z, start)

    acc[...] = jnp.zeros_like(acc)
    top[...] = jnp.full_like(top, NEG_BIG)
    vaug[:, :, HD:] = jnp.ones((groups, block, HD), jnp.bfloat16)
    q_in.wait()

    total_keys = panel * wide * 2
    total_queries = rows * wide * 2
    first_query = total_keys - total_queries + mine * rows
    lane = lax.broadcasted_iota(jnp.int32, (rows, block), 1)
    query_pos = first_query + lax.broadcasted_iota(jnp.int32, (rows, block), 0)

    def by_panel(ref, b):
        got = jnp.full((rows, block), ref[b * 4], jnp.int32)
        for j in range(1, 4):
            got = jnp.where(lane >= j * panel, ref[b * 4 + j], got)
        return got

    def compute(b):
        key_pos = by_panel(order, b) * panel + lane % panel
        bias = jnp.where(key_pos <= query_pos, 0.0, NEG_BIG)
        scale = jnp.exp2(by_panel(key_exp, b)[:8].astype(jnp.float32))
        scale = scale.astype(jnp.bfloat16).astype(jnp.float32)[:1] * (HD**-0.5 * math.log2(math.e))
        first = pl.multiple_of(b * block, block)
        for j in range(4):
            value_scale = jnp.full((16, HD), value_exp[b * 4 + j], jnp.int32).astype(jnp.float32)
            value_scale = jnp.exp2(value_scale).astype(jnp.bfloat16)[:1]
            for g in range(groups):
                value_rows = kv[pl.ds(first + j * panel, panel), width + g * HD : width + (g + 1) * HD]
                vaug[g, j * panel : (j + 1) * panel, :HD] = value_rows * value_scale
        for g in range(groups):
            key_rows = kv[pl.ds(first, block), g * HD : (g + 1) * HD]
            for e in range(g * per_group, (g + 1) * per_group, TILE_HEADS):
                heads = range(e, e + TILE_HEADS)
                span = pl.ds(e * rows, TILE_HEADS * rows)
                q = jnp.concatenate([qv[:, h * HD : (h + 1) * HD] for h in heads], axis=0)
                s = lax.dot_general(
                    q, key_rows, (((1,), (1,)), ((), ())), preferred_element_type=jnp.float32
                )
                s = s.reshape(TILE_HEADS, rows, block) * scale[None] + bias[None]
                s = s.reshape(TILE_HEADS * rows, block)
                old = top[span]
                new = jnp.maximum(old, jnp.max(s, axis=1, keepdims=True))
                top[span] = new
                fade = jnp.exp2(old - new)
                weights = jnp.exp2(s - jnp.concatenate([new] * (block // HD), axis=1))
                mixed = jnp.dot(
                    weights.astype(jnp.bfloat16), vaug[g], preferred_element_type=jnp.float32
                )
                acc[span] = acc[span] * jnp.concatenate([fade, fade], axis=1) + mixed

    below = z < outer - 1 - z
    near = jnp.where(below, z, outer - 1 - z)

    def step(t, carry):
        d = t + 1

        @pl.when(z - d >= 0)
        def _():
            arrived(slot(jnp.maximum(z - d, 0), y, ka))
            each_way(jnp.maximum(z - d, 0), start)

        @pl.when(z + d < outer)
        def _():
            arrived(slot(jnp.minimum(z + d, outer - 1), y, ka))
            each_way(jnp.minimum(z + d, outer - 1), start)

        half = (t + 1) // 2
        both = jnp.where(t % 2 == 1, z + half, z - half)
        rest = jnp.where(below, z + (t - near), z - (t - near))
        b = jnp.where(t <= 2 * near, both, rest)
        arrived(slot(b, 1 - y, ka))
        across(b).start()
        arrived(slot(b, y, 1 - ka))
        arrived(slot(b, 1 - y, 1 - ka))
        compute(b)
        return carry

    lax.fori_loop(0, outer, step, 0)

    for g in range(groups):
        for e in range(g * per_group, (g + 1) * per_group):
            part = acc[pl.ds(e * rows, rows)]
            ov[:, e * HD : (e + 1) * HD] = (part[:, :HD] / part[:, HD:]).astype(jnp.bfloat16)
        columns = pl.ds(g * per_group * HD, per_group * HD)
        pltpu.make_async_copy(ov.at[:, columns], o_hbm.at[:, columns], out_sem.at[g]).start()

    def finish(zz, carry):
        each_way(zz, lambda copy: copy.wait_send())
        across(zz).wait_send()
        return carry

    lax.fori_loop(0, outer, finish, 0)
    for g in range(groups):
        columns = pl.ds(g * per_group * HD, per_group * HD)
        pltpu.make_async_copy(ov.at[:, columns], o_hbm.at[:, columns], out_sem.at[g]).wait()


def local(queries, keys, values, panel_order, key_exp, value_exp):
    rows, columns = queries.shape
    panel, width = keys.shape
    wide = lax.axis_size("pb")
    panels = wide * lax.axis_size("ka")
    heads = columns // HD
    groups = width // HD
    smem = pl.BlockSpec(memory_space=pltpu.SMEM)
    hbm = pl.BlockSpec(memory_space=pl.ANY)
    return pl.pallas_call(
        functools.partial(kernel, wide),
        out_shape=jax.ShapeDtypeStruct((rows, columns), jnp.bfloat16),
        in_specs=[hbm, hbm, hbm, smem, smem, smem],
        out_specs=hbm,
        scratch_shapes=[
            pltpu.VMEM((rows, columns), jnp.bfloat16),
            pltpu.VMEM((panels * panel, 2 * width), jnp.bfloat16),
            pltpu.VMEM((rows, columns), jnp.bfloat16),
            pltpu.VMEM((heads * rows, 2 * HD), jnp.float32),
            pltpu.VMEM((heads * rows, HD), jnp.float32),
            pltpu.VMEM((groups, 4 * panel, 2 * HD), jnp.bfloat16),
            pltpu.SemaphoreType.DMA((3,)),
            pltpu.SemaphoreType.DMA((groups,)),
            pltpu.SemaphoreType.DMA((panels, 4)),
            pltpu.SemaphoreType.DMA((panels,)),
        ],
        compiler_params=pltpu.CompilerParams(
            collective_id=0, has_side_effects=True, vmem_limit_bytes=56 * 1024 * 1024
        ),
        cost_estimate=pl.CostEstimate(
            flops=4 * rows * columns * panels * panel,
            bytes_accessed=4 * rows * columns + 4 * panel * width,
            transcendentals=rows * heads * panels * panel,
        ),
    )(queries, keys, values, panel_order, key_exp, value_exp)


def solution(mesh):
    placed = (
        P(("grp", "pb", "ka"), None),
        P(("grp", "pb", "ka"), None),
        P(("grp", "pb", "ka"), None),
        P("grp"),
        P("grp"),
        P("grp"),
    )
    return jax.shard_map(
        local, mesh=mesh, in_specs=placed, out_specs=P(("grp", "pb", "ka"), None), check_vma=False
    )
```

```python
import functools
import math

import jax
import jax.numpy as jnp
from jax import lax
from jax.experimental import pallas as pl
from jax.experimental.pallas import tpu as pltpu
from jax.sharding import PartitionSpec as P

HD = 128
NEG_BIG = -1e30
MESH = pl.DeviceIdType.MESH
TILE_HEADS = 8
PIECE = 16


def kernel(
    wide, q_hbm, k_hbm, v_hbm, order, key_exp, value_exp, o_hbm,
    qv, kv, ov, acc, top, vaug, hide, factor, in_sem, out_sem, send_sem, recv_sem,
):
    rows = qv.shape[0]
    panel = k_hbm.shape[0]
    width = k_hbm.shape[1]
    groups = width // HD
    per_group = qv.shape[1] // width
    outer = wide // 2
    block = 4 * panel
    pieces = panel // PIECE
    pb, ka = lax.axis_index("pb"), lax.axis_index("ka")
    z, y = pb // 2, pb % 2

    def slot(zz, yy, kk):
        return (zz * 2 + yy) * 2 + kk

    def at(s, p=None):
        if p is None:
            return kv.at[pl.ds(pl.multiple_of(s * panel, panel), panel)]
        return kv.at[pl.ds(pl.multiple_of(s * panel + p * PIECE, PIECE), PIECE)]

    def remote(s, p, way, to_pb, to_ka):
        land = 0 if way == 3 or p is None else p
        return pltpu.make_async_remote_copy(
            src_ref=at(s, p), dst_ref=at(s, p),
            send_sem=send_sem.at[s, way], recv_sem=recv_sem.at[s, land],
            device_id={"pb": to_pb, "ka": to_ka}, device_id_type=MESH,
        )

    def each_way(zz, p, act):
        s = slot(zz, y, ka)

        @pl.when((zz <= z) & (z + 1 < outer))
        def _():
            act(remote(s, p, 0, jnp.minimum(pb + 2, wide - 1), ka))

        @pl.when((zz >= z) & (z >= 1))
        def _():
            act(remote(s, p, 1, jnp.maximum(pb - 2, 0), ka))

        act(remote(s, p, 2, z * 2 + 1 - y, ka))
        act(remote(s, p, 3, pb, 1 - ka))

    def across(zz, p):
        return remote(slot(zz, 1 - y, ka), p, 3, pb, 1 - ka)

    def arrived(s, p):
        remote(s, p, 2, pb, 1 - ka).wait_recv()

    def start(copy):
        copy.start()

    mine = slot(z, y, ka)
    k_in = pltpu.make_async_copy(k_hbm, at(mine).at[:, pl.ds(0, width)], in_sem.at[0])
    v_in = pltpu.make_async_copy(v_hbm, at(mine).at[:, pl.ds(width, width)], in_sem.at[1])
    q_in = pltpu.make_async_copy(q_hbm, qv, in_sem.at[2])
    k_in.start()
    v_in.start()
    q_in.start()

    barrier = pltpu.get_barrier_semaphore()
    pl.semaphore_signal(barrier, inc=1, device_id={"pb": pb, "ka": 1 - ka}, device_id_type=MESH)
    pl.semaphore_signal(
        barrier, inc=1, device_id={"pb": z * 2 + 1 - y, "ka": ka}, device_id_type=MESH
    )

    @pl.when(z + 1 < outer)
    def _():
        pl.semaphore_signal(
            barrier, inc=1, device_id={"pb": jnp.minimum(pb + 2, wide - 1), "ka": ka},
            device_id_type=MESH,
        )

    @pl.when(z >= 1)
    def _():
        pl.semaphore_signal(
            barrier, inc=1, device_id={"pb": jnp.maximum(pb - 2, 0), "ka": ka}, device_id_type=MESH
        )

    inside = (z + 1 < outer).astype(jnp.int32) + (z >= 1).astype(jnp.int32)
    pl.semaphore_wait(barrier, 2 + inside)

    k_in.wait()
    v_in.wait()
    for p in range(pieces):
        each_way(z, p, start)

    acc[...] = jnp.zeros_like(acc)
    top[...] = jnp.full_like(top, NEG_BIG)
    vaug[:, :, HD:] = jnp.ones((groups, block, HD), jnp.bfloat16)
    q_in.wait()

    total_keys = panel * wide * 2
    total_queries = rows * wide * 2
    first_query = total_keys - total_queries + mine * rows
    lane = lax.broadcasted_iota(jnp.int32, (rows, block), 1)
    query_pos = first_query + lax.broadcasted_iota(jnp.int32, (rows, block), 0)

    def by_panel(ref, b):
        got = jnp.full((rows, block), ref[b * 4], jnp.int32)
        for j in range(1, 4):
            got = jnp.where(lane >= j * panel, ref[b * 4 + j], got)
        return got

    def prepare(b):
        key_pos = by_panel(order, b) * panel + lane % panel
        hide[...] = jnp.where(key_pos <= query_pos, 0.0, NEG_BIG)
        scale = jnp.exp2(by_panel(key_exp, b)[:8].astype(jnp.float32))
        scale = scale.astype(jnp.bfloat16).astype(jnp.float32)
        factor[...] = scale * (HD**-0.5 * math.log2(math.e))

    def compute(b, g):
        first = pl.multiple_of(b * block, block)
        for j in range(4):
            value_scale = jnp.full((16, HD), value_exp[b * 4 + j], jnp.int32).astype(jnp.float32)
            value_scale = jnp.exp2(value_scale).astype(jnp.bfloat16)[:1]
            value_rows = kv[pl.ds(first + j * panel, panel), width + g * HD : width + (g + 1) * HD]
            vaug[g, j * panel : (j + 1) * panel, :HD] = value_rows * value_scale
        key_rows = kv[pl.ds(first, block), g * HD : (g + 1) * HD]
        for e in range(g * per_group, (g + 1) * per_group, TILE_HEADS):
            heads = range(e, e + TILE_HEADS)
            span = pl.ds(e * rows, TILE_HEADS * rows)
            q = jnp.concatenate([qv[:, h * HD : (h + 1) * HD] for h in heads], axis=0)
            s = lax.dot_general(
                q, key_rows, (((1,), (1,)), ((), ())), preferred_element_type=jnp.float32
            )
            s = s.reshape(TILE_HEADS, rows, block) * factor[:1][None] + hide[...][None]
            s = s.reshape(TILE_HEADS * rows, block)
            old = top[span]
            new = jnp.maximum(old, jnp.max(s, axis=1, keepdims=True))
            top[span] = new
            fade = jnp.exp2(old - new)
            weights = jnp.exp2(s - jnp.concatenate([new] * (block // HD), axis=1))
            mixed = jnp.dot(
                weights.astype(jnp.bfloat16), vaug[g], preferred_element_type=jnp.float32
            )
            acc[span] = acc[span] * jnp.concatenate([fade, fade], axis=1) + mixed

    def out_copy(g):
        columns = pl.ds(g * per_group * HD, per_group * HD)
        return pltpu.make_async_copy(ov.at[:, columns], o_hbm.at[:, columns], out_sem.at[g])

    def conclude(g):
        for e in range(g * per_group, (g + 1) * per_group):
            part = acc[pl.ds(e * rows, rows)]
            ov[:, e * HD : (e + 1) * HD] = (part[:, :HD] / part[:, HD:]).astype(jnp.bfloat16)
        out_copy(g).start()

    below = z < outer - 1 - z
    near = jnp.where(below, z, outer - 1 - z)

    def nth(t):
        half = (t + 1) // 2
        both = jnp.where(t % 2 == 1, z + half, z - half)
        rest = jnp.where(below, z + (t - near), z - (t - near))
        return jnp.clip(jnp.where(t <= 2 * near, both, rest), 0, outer - 1)

    def step(u, carry, last=False):
        d = u + 1
        b = nth(u)
        for p in range(pieces):

            @pl.when(z - d >= 0)
            def _():
                zz = jnp.maximum(z - d, 0)
                arrived(slot(zz, y, ka), p)
                each_way(zz, p, start)

            @pl.when(z + d < outer)
            def _():
                zz = jnp.minimum(z + d, outer - 1)
                arrived(slot(zz, y, ka), p)
                each_way(zz, p, start)

        for p in range(pieces):
            arrived(slot(b, 1 - y, ka), p)
            across(b, p).start()
        prepare(b)
        arrived(slot(b, y, 1 - ka), None)
        arrived(slot(b, 1 - y, 1 - ka), None)
        for g in range(groups):
            compute(b, g)
            if last:
                conclude(g)
        return carry

    lax.fori_loop(0, outer - 1, step, 0)
    step(outer - 1, 0, last=True)

    def finish(zz, carry):
        each_way(zz, None, lambda copy: copy.wait_send())
        across(zz, None).wait_send()
        return carry

    lax.fori_loop(0, outer, finish, 0)
    for g in range(groups):
        out_copy(g).wait()


def local(queries, keys, values, panel_order, key_exp, value_exp):
    rows, columns = queries.shape
    panel, width = keys.shape
    wide = lax.axis_size("pb")
    panels = wide * lax.axis_size("ka")
    heads = columns // HD
    groups = width // HD
    smem = pl.BlockSpec(memory_space=pltpu.SMEM)
    hbm = pl.BlockSpec(memory_space=pl.ANY)
    return pl.pallas_call(
        functools.partial(kernel, wide),
        out_shape=jax.ShapeDtypeStruct((rows, columns), jnp.bfloat16),
        in_specs=[hbm, hbm, hbm, smem, smem, smem],
        out_specs=hbm,
        scratch_shapes=[
            pltpu.VMEM((rows, columns), jnp.bfloat16),
            pltpu.VMEM((panels * panel, 2 * width), jnp.bfloat16),
            pltpu.VMEM((rows, columns), jnp.bfloat16),
            pltpu.VMEM((heads * rows, 2 * HD), jnp.float32),
            pltpu.VMEM((heads * rows, HD), jnp.float32),
            pltpu.VMEM((groups, 4 * panel, 2 * HD), jnp.bfloat16),
            pltpu.VMEM((rows, 4 * panel), jnp.float32),
            pltpu.VMEM((8, 4 * panel), jnp.float32),
            pltpu.SemaphoreType.DMA((3,)),
            pltpu.SemaphoreType.DMA((groups,)),
            pltpu.SemaphoreType.DMA((panels, 4)),
            pltpu.SemaphoreType.DMA((panels, panel // PIECE)),
        ],
        compiler_params=pltpu.CompilerParams(
            collective_id=0, has_side_effects=True, vmem_limit_bytes=56 * 1024 * 1024
        ),
        cost_estimate=pl.CostEstimate(
            flops=4 * rows * columns * panels * panel,
            bytes_accessed=4 * rows * columns + 4 * panel * width,
            transcendentals=rows * heads * panels * panel,
        ),
    )(queries, keys, values, panel_order, key_exp, value_exp)


def solution(mesh):
    placed = (
        P(("grp", "pb", "ka"), None),
        P(("grp", "pb", "ka"), None),
        P(("grp", "pb", "ka"), None),
        P("grp"),
        P("grp"),
        P("grp"),
    )
    return jax.shard_map(
        local, mesh=mesh, in_specs=placed, out_specs=P(("grp", "pb", "ka"), None), check_vma=False
    )
```
